32 devices in a mesh: table: 4 (over x, core), row: 8 (over z, y).
Axes of the slice: x: 2, y: 2, z: 4, core: 2. Of those that a mesh axis runs over, the one named last changes fastest.
Arguments:
- features: bfloat16 [4096, 4096], P('row', 'table'), may hold values from -6 to 6
- cotangent: bfloat16 [4096, 4096], P('row', 'table'), may hold values from -6 to 6
- cross_in: bfloat16 [4096, 512], P('table'), may hold values from -0.09375 to 0.09375
- cross_out: bfloat16 [4096, 512], P('table'), may hold values from -0.25 to 0.25
- bias: float32 [4096], P('table'), may hold values from -6 to 6
- dest_shard: int32 [32, 4096, 1], P('table', 'row'), may hold values from 0 to 7; in each aligned block of 512 rows (0 to 511, 512 to 1023, ..., all dimensions but the last counted through in order) at most 96 rows name the same one
- quot_row: int32 [32, 4096], P('table', 'row'), may hold values from 0 to 1023
- rem_row: int32 [32, 4096], P('table', 'row'), may hold values from 0 to 2047
- quot_slab: bfloat16 [32, 8192, 128], P('table', 'row'), may hold values from -6 to 6
- quot_accum: float32 [32, 8192], P('table', 'row'), may hold values from 0.05 to 2
- rem_table: bfloat16 [32, 2048, 128], P('table'), may hold values from -6 to 6
- rem_accum: float32 [32, 2048], P('table'), may hold values from 0.5 to 20
Outputs:
- quot_out: bfloat16 [32, 8192, 128], P('table', 'row')
- quot_acc_out: float32 [32, 8192], P('table', 'row')
- rem_out: bfloat16 [32, 2048, 128], P('table')
- rem_acc_out: float32 [32, 2048], P('table', 'row')
The draws below stay inside these ranges and needn't reach their ends.
Inputs may be any that keep to these rules, and one draw needn't show every extreme that they name: `dest_shard`: for each table, the 512 samples of one index of row name one row shard at most 96 times, a bound that some block reaches.
All inputs are finite; a program needn't handle non-finite values.
Results may differ from the reference program's by a relative error of at most 0.004.
Values may be sent and summed in bfloat16 or wider, within the bound.
A program may use at most 128 MiB of HBM per device.

```python
import math
import jax
import jax.numpy as jnp
import numpy as np
from jax import lax

EMB = 128
RANK = 512
REM = 2048
QR_DEV = 1024
B_DEV = 512
TABLES = 32
D = 4096
B = 4096
QROWS = 8192
CAP = 96
N_ROW = 8


def place_ends(drawn, rng, smallest, top_value):
    longest = drawn.shape.index(max(drawn.shape))
    spots = []
    for shift in (0, 1):
        where = [jax.random.randint(jax.random.fold_in(rng, axis), (), 0, length) for axis, length in enumerate(drawn.shape)]
        where[longest] = (where[longest] + shift) % drawn.shape[longest]
        spots.append(tuple(where))
    return drawn.at[spots[0]].set(smallest).at[spots[1]].set(top_value)


def shard_levels(rng, extent, pieces, least, top_value):
    def one(dim, shards_of):
        steps = jax.random.uniform(jax.random.fold_in(jax.random.fold_in(rng, 6), dim), (shards_of,), jnp.float32, least / len(pieces), top_value / len(pieces))
        return jnp.repeat(jnp.exp(steps), extent[dim] // shards_of).reshape((-1,) + (1,) * (len(extent) - dim - 1))

    gain = one(*pieces[0])
    for cut in pieces[1:]:
        gain = gain * one(*cut)
    return gain


def deal_out(stream_key, own, number, rows, number_of, top, limit, skew):
    sequence = jax.random.permutation(stream_key, number_of)
    heavy_load, usual = shares(number_of, rows * top, limit, skew, True), shares(number_of, rows * top, limit, skew, False)
    places = jnp.arange(number_of)

    def named(sizes, offset_by):
        used = int((sizes > 0).sum())
        fixed = max(1, used // 4)
        moved = fixed + (places - fixed + offset_by * (used - fixed)) % max(1, number_of - fixed)
        return jnp.zeros((number_of,), jnp.int32).at[sequence[jnp.where(places < fixed, places, moved)]].set(jnp.asarray(sizes, jnp.int32))

    sizes = jnp.where(number % 4 == 0, named(heavy_load, number // 4), named(usual, number - number // 4 - 1))
    mixed = jax.random.permutation(jax.random.fold_in(own, 3), number_of)
    source_of, receiver = mixed[0:number_of // 2 * 2:2], mixed[1:number_of // 2 * 2:2]
    room = jnp.minimum(sizes[source_of] - 1, limit - sizes[receiver]) // 2
    room = jnp.where((source_of == sequence[0]) | (receiver == sequence[0]) | (sizes[receiver] == 0), 0, jnp.maximum(room, 0))
    moved = jax.random.randint(jax.random.fold_in(own, 4), (number_of // 2,), 0, 1 << 20) % (room + 1)
    sizes = sizes.at[source_of].add(-moved).at[receiver].add(moved)
    labels = jnp.searchsorted(jnp.cumsum(sizes), jnp.arange(rows * top), side="right").astype(jnp.int32)
    listing = labels.reshape(top, rows).T
    listing = listing[jax.random.permutation(jax.random.fold_in(own, 1), rows)]
    offset_by = jax.random.randint(jax.random.fold_in(own, 2), (rows, 1), 0, top)
    return jnp.take_along_axis(listing, (jnp.arange(top)[None, :] + offset_by) % top, axis=1)


def shares(count, total, bound, slope, full):
    loads = [(1 << 20) // math.isqrt(rank ** slope) + 1 for rank in range(1, count + 1)]
    largest = bound if full else min(bound, max(-(-total // count), total * loads[0] // sum(loads)))
    least = 1 if total - largest >= count - 1 else 0
    given, rest = [largest] + [least] * (count - 1), total - largest - least * (count - 1)
    while rest > 0:
        free = [i for i in range(1, count) if given[i] < largest] or [i for i in range(1, count) if given[i] < bound]
        mass, left = sum([loads[i] for i in free]), rest
        for i in free:
            extra = min(bound - given[i], max(1, left * loads[i] // mass), rest)
            given[i] = given[i] + extra
            rest = rest - extra
    return np.array(given)


def normal_values(rng, shape, scale, bound, cuts=(), kind=jnp.bfloat16):
    level = shard_levels(rng, shape, cuts, -0.22, 0.18) if cuts else 1.0
    result = jax.random.normal(rng, shape, jnp.float32) * scale * level
    return jnp.minimum(jnp.maximum(result, -bound), bound).astype(kind)


def setup_inputs(seed: int = 0) -> dict:
    splits = jax.random.split(jax.random.key(seed), 13)
    features = normal_values(splits[0], (B, D), 1.0, 6.0, ((0, 8), (1, 4)))
    cotangent = normal_values(splits[1], (B, D), 1.0, 6.0, ((0, 8), (1, 4)))
    cross_in = normal_values(splits[2], (D, RANK), D ** -0.5, 0.09375, ((0, 4),))
    cross_out = normal_values(splits[3], (D, RANK), RANK ** -0.5, 0.25, ((0, 4),))
    bias = normal_values(splits[4], (D,), 1.0, 6.0, ((0, 4),), jnp.float32)
    dest_shard_keys = jax.random.split(jax.random.fold_in(splits[5], 1), TABLES * B // B_DEV)
    dest_shard_turns = jax.random.permutation(jax.random.fold_in(splits[5], 3), TABLES * B // B_DEV)
    dest_shard = jax.vmap(lambda own, number: deal_out(jax.random.fold_in(splits[5], 2), own, number, B_DEV, N_ROW, 1, CAP, 2))(dest_shard_keys, dest_shard_turns).reshape((TABLES, B, 1))
    quot_row = place_ends(jax.random.randint(splits[6], (TABLES, B), 0, QR_DEV), jax.random.fold_in(splits[6], 1), 0, QR_DEV - 1).astype(jnp.int32)
    rem_row = place_ends(jax.random.randint(splits[7], (TABLES, B), 0, REM), jax.random.fold_in(splits[7], 1), 0, REM - 1).astype(jnp.int32)
    quot_slab = normal_values(splits[8], (TABLES, QROWS, EMB), 1.0, 6.0, ((0, 4), (1, 8)))
    quot_accum = jnp.clip(jnp.exp(math.log(2.0) - 3.6888794 * jax.random.uniform(splits[9], (TABLES, QROWS), jnp.float32) ** shard_levels(splits[9], (TABLES, QROWS), ((0, 4), (1, 8)), -0.2, 0.2)), 0.05, 2.0)
    rem_table = normal_values(splits[10], (TABLES, REM, EMB), 1.0, 6.0, ((0, 4),))
    rem_accum = jnp.clip(jnp.exp(math.log(20.0) - 3.6888795 * jax.random.uniform(splits[11], (TABLES, REM), jnp.float32) ** shard_levels(splits[11], (TABLES, REM), ((0, 4),), -0.2, 0.2)), 0.5, 20.0)
    return {"features": features, "cotangent": cotangent, "cross_in": cross_in, "cross_out": cross_out, "bias": bias, "dest_shard": dest_shard, "quot_row": quot_row, "rem_row": rem_row, "quot_slab": quot_slab, "quot_accum": quot_accum, "rem_table": rem_table, "rem_accum": rem_accum}


step_rate = 0.3
epsilon = 1e-06

def reference(features, cotangent, cross_in, cross_out, bias, dest_shard, quot_row, rem_row, quot_slab, quot_accum, rem_table, rem_accum):
    contract = (((1,), (1,)), ((), ()))

    def one_block(block):
        feats, cotan = block
        product = (cotan.astype(jnp.float32) * feats.astype(jnp.float32)).astype(jnp.bfloat16)
        rank_left = jnp.dot(feats, cross_in, preferred_element_type=jnp.float32).astype(jnp.bfloat16)
        rank_right = jnp.dot(product, cross_out, preferred_element_type=jnp.float32).astype(jnp.bfloat16)
        cross_gate = lax.dot_general(rank_left, cross_out, contract, preferred_element_type=jnp.float32) + bias
        cross_back = lax.dot_general(rank_right, cross_in, contract, preferred_element_type=jnp.float32)
        return (cotan.astype(jnp.float32) * (cross_gate + 1.0) + cross_back).astype(jnp.bfloat16)
    pooled = lax.map(one_block, (features.reshape(N_ROW, B_DEV, D), cotangent.reshape(N_ROW, B_DEV, D)))
    pooled = pooled.reshape(B, TABLES, EMB).transpose(1, 0, 2)

    def one_table(items):
        grads, target, qlocal, rlocal, slab, rtab = items
        qindex = target[:, 0] * QR_DEV + qlocal
        grad_q = jax.ops.segment_sum(grads.astype(jnp.float32) * rtab[rlocal].astype(jnp.float32), qindex, num_segments=QR_DEV * N_ROW)
        grad_r = jax.ops.segment_sum(grads.astype(jnp.float32) * slab[qindex].astype(jnp.float32), rlocal, num_segments=REM)
        return (grad_q, grad_r)
    quot_grad, rem_grad = lax.map(one_table, (pooled, dest_shard, quot_row, rem_row, quot_slab, rem_table))
    quot_acc_out = quot_accum + lax.optimization_barrier(jnp.mean(quot_grad * quot_grad, axis=-1))
    quot_out = (quot_slab.astype(jnp.float32) - step_rate * quot_grad * lax.rsqrt(quot_acc_out + epsilon)[..., None]).astype(jnp.bfloat16)
    rem_acc_out = rem_accum + lax.optimization_barrier(jnp.mean(rem_grad * rem_grad, axis=-1))
    rem_out = (rem_table.astype(jnp.float32) - step_rate * rem_grad * lax.rsqrt(rem_acc_out + epsilon)[..., None]).astype(jnp.bfloat16)
    return (quot_out, quot_acc_out, rem_out, rem_acc_out)
```

```python
import functools

import jax
import jax.numpy as jnp
from jax import lax
from jax.experimental import pallas as pl
from jax.experimental.pallas import tpu as pltpu
from jax.sharding import PartitionSpec as P

step_rate = 0.3
epsilon = 1e-06
MESH = pl.DeviceIdType.MESH


def enter(axis, size):
    me = lax.axis_index(axis)
    barrier = pltpu.get_barrier_semaphore()
    for hop in range(1, size):
        pl.semaphore_signal(
            barrier, inc=1, device_id={axis: lax.rem(me + hop, size)}, device_id_type=MESH
        )
    pl.semaphore_wait(barrier, size - 1)


def digits(me, levels):
    return [lax.rem(me // (1 << b), 2) for b in range(levels)]


def across(me, bit, b):
    return me + (1 - 2 * bit) * (1 << b)


def one_hot(wanted, first, shape, axis):
    names = lax.broadcasted_iota(jnp.int32, shape, axis) + first
    return jnp.where(names == wanted, 1.0, 0.0).astype(jnp.bfloat16)


def tables_kernel(
    n,
    levels,
    send_ref,
    cols_ref,
    rows_ref,
    slab_ref,
    qacc_ref,
    rem_ref,
    racc_ref,
    quot_ref,
    qacc_out_ref,
    rem_out_ref,
    racc_out_ref,
    got,
    part,
    *rest,
):
    held = list(rest[: levels - 1])
    landed = list(rest[levels - 1 : 2 * levels - 1])
    deal_send, deal_recv, send_sem, recv_sem = rest[2 * levels - 1 :]
    me = lax.axis_index("row")
    bits = digits(me, levels)
    tables, _, capacity, width = send_ref.shape
    slots = n * capacity
    rem_rows = rem_ref.shape[1]
    quot_rows = slab_ref.shape[1]
    share = rem_rows // n
    every = slice(None)
    stages = [part] + held

    def deal(t, hop):
        return pltpu.make_async_remote_copy(
            src_ref=send_ref.at[t, lax.rem(me + hop, n)],
            dst_ref=got.at[t, me],
            send_sem=deal_send.at[t, hop - 1],
            recv_sem=deal_recv.at[t, hop - 1],
            device_id={"row": lax.rem(me + hop, n)},
            device_id_type=MESH,
        )

    def halve(t, b):
        where = (t,) + (every,) * (levels - b - 1) + (1 - bits[b],)
        return pltpu.make_async_remote_copy(
            src_ref=stages[b].at[where],
            dst_ref=landed[b].at[t],
            send_sem=send_sem.at[b, t],
            recv_sem=recv_sem.at[b, t],
            device_id={"row": across(me, bits[b], b)},
            device_id_type=MESH,
        )

    def spread(t, b):
        where = (t,) + (every,) * (levels - b - 1) + tuple(bits[c] for c in range(b, -1, -1))
        return pltpu.make_async_remote_copy(
            src_ref=rem_out_ref.at[where],
            dst_ref=rem_out_ref.at[where],
            send_sem=send_sem.at[levels + b, t],
            recv_sem=recv_sem.at[levels + b, t],
            device_id={"row": across(me, bits[b], b)},
            device_id_type=MESH,
        )

    enter("row", n)

    def start_deal(t, carry):
        for hop in range(1, n):
            deal(t, hop).start()
        return carry

    lax.fori_loop(0, tables, start_deal, 0)

    def pick(wanted, table_ref, t, count):
        total = jnp.zeros((slots, width), jnp.float32)
        chunk = min(count, 512)
        for first in range(0, count, chunk):
            hot = one_hot(wanted, first, (slots, chunk), 1)
            total += jnp.dot(
                hot, table_ref[t, pl.ds(first, chunk), :], preferred_element_type=jnp.float32
            )
        return total

    def table_step(t):
        got[t, me] = send_ref[t, me]
        for hop in range(1, n):
            deal(t, hop).wait_recv()
        grads = got[t].reshape(slots, width).astype(jnp.float32)
        cols = cols_ref[t]
        rows = rows_ref[t]
        quot_pick = pick(cols[:, 0:1], slab_ref, t, quot_rows)
        for_rem = (grads * quot_pick).astype(jnp.bfloat16)
        chunk = max(share, 512)
        for first in range(0, rem_rows, chunk):
            hot = one_hot(rows[1:2, :], first, (chunk, slots), 0)
            grad = jnp.dot(hot, for_rem, preferred_element_type=jnp.float32)
            for r in range(first // share, (first + chunk) // share):
                where = tuple((r >> b) & 1 for b in range(levels - 1, -1, -1))
                part[(t,) + where] = grad[r * share - first : (r + 1) * share - first].astype(
                    jnp.bfloat16
                )
        halve(t, 0).start()
        rem_pick = pick(cols[:, 1:2], rem_ref, t, rem_rows)
        for_quot = (grads * rem_pick).astype(jnp.bfloat16)
        chunk = min(quot_rows, 512)
        for first in range(0, quot_rows, chunk):
            here = pl.ds(first, chunk)
            hot = one_hot(rows[0:1, :], first, (chunk, slots), 0)
            grad = jnp.dot(hot, for_quot, preferred_element_type=jnp.float32)
            fresh, fresh_acc = adagrad(slab_ref[t, here, :], qacc_ref[t, :, here], grad)
            quot_ref[t, here, :] = fresh
            qacc_out_ref[t, :, here] = fresh_acc

    def adagrad(old, accum, grad):
        count = old.shape[0]
        mean = jnp.mean(grad * grad, axis=-1, keepdims=True)
        fresh_acc = jnp.broadcast_to(accum, (width, count)).T + mean
        fresh = old.astype(jnp.float32) - step_rate * grad * lax.rsqrt(fresh_acc + epsilon)
        return fresh.astype(jnp.bfloat16), fresh_acc.T[0:1, :]

    def sum_of(t, b, where):
        kept = stages[b][(t,) + where + (bits[b],)].astype(jnp.float32)
        return kept + landed[b][(t,) + where].astype(jnp.float32)

    def comm_step(t, s):
        if s <= levels:
            halve(t, s - 1).wait_recv()
            if s < levels:
                for i in range(1 << (levels - s)):
                    where = tuple((i >> b) & 1 for b in range(levels - s - 1, -1, -1))
                    held[s - 1][(t,) + where] = sum_of(t, s - 1, where).astype(jnp.bfloat16)
                halve(t, s).start()
            else:
                old = rem_ref[t, pl.ds(pl.multiple_of(me * share, share), share), :]
                fresh, fresh_acc = adagrad(old, racc_ref[t], sum_of(t, s - 1, ()))
                rem_out_ref[(t,) + tuple(bits[::-1])] = fresh
                racc_out_ref[t] = fresh_acc
                spread(t, levels - 1).start()
        else:
            b = 2 * levels - s
            spread(t, b).wait_recv()
            if b > 0:
                spread(t, b - 1).start()

    def step(i, carry):
        @pl.when(i < tables)
        def _():
            table_step(i)

        for s in range(2 * levels, 0, -1):
            t = i - s

            @pl.when((t >= 0) & (t < tables))
            def _():
                comm_step(t, s)

        return carry

    lax.fori_loop(0, tables + 2 * levels, step, 0)

    def finish(t, carry):
        for hop in range(1, n):
            deal(t, hop).wait_send()
        for b in range(levels):
            halve(t, b).wait_send()
            spread(t, b).wait_send()
        return carry

    lax.fori_loop(0, tables, finish, 0)


def tables_call(send_rows, keys, slab, qacc, rem_table, rem_accum):
    tables, n, capacity, width = send_rows.shape
    levels = n.bit_length() - 1
    rem_rows, quot_rows = rem_table.shape[1], slab.shape[1]
    share = rem_rows // n
    both = jnp.stack((keys // rem_rows, keys % rem_rows), axis=1)
    own_acc = lax.dynamic_slice_in_dim(rem_accum, lax.axis_index("row") * share, share, 1)
    vmem = pl.BlockSpec(memory_space=pltpu.VMEM)
    cube = lambda b: (tables,) + (2,) * b + (share, width)
    outs = pl.pallas_call(
        functools.partial(tables_kernel, n, levels),
        out_shape=(
            jax.ShapeDtypeStruct(slab.shape, jnp.bfloat16),
            jax.ShapeDtypeStruct((tables, 1, quot_rows), jnp.float32),
            jax.ShapeDtypeStruct(cube(levels), jnp.bfloat16),
            jax.ShapeDtypeStruct((tables, 1, share), jnp.float32),
        ),
        in_specs=[vmem] * 7,
        out_specs=(vmem,) * 4,
        scratch_shapes=[pltpu.VMEM((tables, n, capacity, width), jnp.bfloat16)]
        + [pltpu.VMEM(cube(b), jnp.bfloat16) for b in range(levels, 0, -1)]
        + [pltpu.VMEM(cube(b), jnp.bfloat16) for b in range(levels - 1, -1, -1)]
        + [pltpu.SemaphoreType.DMA((tables, n - 1))] * 2
        + [pltpu.SemaphoreType.DMA((2 * levels, tables))] * 2,
        compiler_params=pltpu.CompilerParams(
            collective_id=0, has_side_effects=True, vmem_limit_bytes=60 << 20
        ),
    )(
        send_rows,
        both.transpose(0, 2, 1),
        both,
        slab,
        qacc[:, None, :],
        rem_table,
        own_acc[:, None, :],
    )
    quot_out, quot_acc_out, rem_out, rem_acc_out = outs
    return (
        quot_out,
        quot_acc_out[:, 0],
        rem_out.reshape(rem_table.shape),
        rem_acc_out[:, 0],
    )


def per_device(
    features,
    cotangent,
    cross_in,
    cross_out,
    bias,
    dest_shard,
    quot_row,
    rem_row,
    quot_slab,
    quot_accum,
    rem_table,
    rem_accum,
):
    contract = (((1,), (1,)), ((), ()))
    samples = features.shape[0]
    tables_dev = quot_slab.shape[0]
    row_width = quot_slab.shape[2]
    rem_rows = rem_table.shape[1]
    row_count = lax.axis_size("row")
    capacity = 3 * samples // (2 * row_count)
    slots = row_count * capacity
    product = (cotangent.astype(jnp.float32) * features.astype(jnp.float32)).astype(jnp.bfloat16)
    rank_left = jnp.dot(features, cross_in, preferred_element_type=jnp.float32)
    rank_right = jnp.dot(product, cross_out, preferred_element_type=jnp.float32)
    rank_left, rank_right = lax.psum((rank_left, rank_right), "table")
    cross_gate = (
        lax.dot_general(
            rank_left.astype(jnp.bfloat16), cross_out, contract, preferred_element_type=jnp.float32
        )
        + bias
    )
    cross_back = lax.dot_general(
        rank_right.astype(jnp.bfloat16), cross_in, contract, preferred_element_type=jnp.float32
    )
    pooled = (cotangent.astype(jnp.float32) * (cross_gate + 1.0) + cross_back).astype(jnp.bfloat16)
    pooled = pooled.reshape(samples, tables_dev, row_width)
    target = dest_shard[:, :, 0]
    onehot = target[:, :, None] == jnp.arange(row_count, dtype=jnp.int32)[None, None, :]
    lower = (
        jnp.arange(samples, dtype=jnp.int32)[:, None]
        >= jnp.arange(samples, dtype=jnp.int32)[None, :]
    ).astype(jnp.bfloat16)
    running = jnp.einsum(
        "ij,tjn->tin", lower, onehot.astype(jnp.bfloat16), preferred_element_type=jnp.float32
    )
    slot_index = jnp.sum(jnp.where(onehot, running, 0.0), axis=2).astype(jnp.int32) - 1
    position = target * capacity + slot_index
    placed = position[:, :, None] == jnp.arange(slots, dtype=jnp.int32)[None, None, :]
    send_rows = jnp.einsum(
        "tsk,ste->tke", placed.astype(jnp.bfloat16), pooled, preferred_element_type=jnp.float32
    ).astype(jnp.bfloat16)
    key_words = quot_row * rem_rows + rem_row
    send_keys = jnp.sum(jnp.where(placed, key_words[:, :, None], 0), axis=1)
    send_rows = send_rows.reshape(tables_dev, row_count, capacity, row_width)
    send_keys = send_keys.reshape(tables_dev, row_count, capacity)
    got_keys = lax.all_to_all(send_keys, "row", split_axis=1, concat_axis=1, tiled=True)
    got_keys = got_keys.reshape(tables_dev, slots)
    return tables_call(send_rows, got_keys, quot_slab, quot_accum, rem_table, rem_accum)


def solution(mesh):
    placed = (
        P("row", "table"),
        P("row", "table"),
        P("table", None),
        P("table", None),
        P("table"),
        P("table", "row", None),
        P("table", "row"),
        P("table", "row"),
        P("table", "row", None),
        P("table", "row"),
        P("table", None, None),
        P("table", None),
    )
    return jax.shard_map(
        per_device,
        mesh=mesh,
        in_specs=placed,
        out_specs=(
            P("table", "row", None),
            P("table", "row"),
            P("table", None, None),
            P("table", "row"),
        ),
        check_vma=False,
    )
```

```python
import functools

import jax
import jax.numpy as jnp
from jax import lax
from jax.experimental import pallas as pl
from jax.experimental.pallas import tpu as pltpu
from jax.sharding import PartitionSpec as P

step_rate = 0.3
epsilon = 1e-06
MESH = pl.DeviceIdType.MESH


def enter(axis, size):
    me = lax.axis_index(axis)
    barrier = pltpu.get_barrier_semaphore()
    for hop in range(1, size):
        pl.semaphore_signal(
            barrier, inc=1, device_id={axis: lax.rem(me + hop, size)}, device_id_type=MESH
        )
    pl.semaphore_wait(barrier, size - 1)


def digits(me, levels):
    return [lax.rem(me // (1 << b), 2) for b in range(levels)]


def across(me, bit, b):
    return me + (1 - 2 * bit) * (1 << b)


def one_hot(wanted, first, shape, axis):
    names = lax.broadcasted_iota(jnp.int32, shape, axis) + first
    return jnp.where(names == wanted, 1.0, 0.0).astype(jnp.bfloat16)


def tables_kernel(
    n,
    levels,
    send_ref,
    rows_ref,
    slab_ref,
    qacc_ref,
    rem_ref,
    racc_ref,
    quot_ref,
    qacc_out_ref,
    rem_out_ref,
    racc_out_ref,
    got,
    part,
    *rest,
):
    held = list(rest[: levels - 1])
    landed = list(rest[levels - 1 : 2 * levels - 1])
    deal_send, deal_recv, send_sem, recv_sem = rest[2 * levels - 1 :]
    me = lax.axis_index("row")
    bits = digits(me, levels)
    tables, _, capacity, width = send_ref.shape
    slots = n * capacity
    rem_rows = rem_ref.shape[1]
    quot_rows = slab_ref.shape[1]
    share = rem_rows // n
    every = slice(None)
    stages = [part] + held

    def deal(t, hop):
        return pltpu.make_async_remote_copy(
            src_ref=send_ref.at[t, lax.rem(me + hop, n)],
            dst_ref=got.at[t, me],
            send_sem=deal_send.at[t, hop - 1],
            recv_sem=deal_recv.at[t, hop - 1],
            device_id={"row": lax.rem(me + hop, n)},
            device_id_type=MESH,
        )

    def halve(t, b):
        where = (t,) + (every,) * (levels - b - 1) + (1 - bits[b],)
        return pltpu.make_async_remote_copy(
            src_ref=stages[b].at[where],
            dst_ref=landed[b].at[t],
            send_sem=send_sem.at[b, t],
            recv_sem=recv_sem.at[b, t],
            device_id={"row": across(me, bits[b], b)},
            device_id_type=MESH,
        )

    def spread(t, b):
        where = (t,) + (every,) * (levels - b - 1) + tuple(bits[c] for c in range(b, -1, -1))
        return pltpu.make_async_remote_copy(
            src_ref=rem_out_ref.at[where],
            dst_ref=rem_out_ref.at[where],
            send_sem=send_sem.at[levels + b, t],
            recv_sem=recv_sem.at[levels + b, t],
            device_id={"row": across(me, bits[b], b)},
            device_id_type=MESH,
        )

    enter("row", n)

    def start_deal(t, carry):
        for hop in range(1, n):
            deal(t, hop).start()
        return carry

    lax.fori_loop(0, tables, start_deal, 0)

    def pick(wanted, table_ref, t, count):
        total = jnp.zeros((slots, width), jnp.float32)
        chunk = min(count, 512)
        for first in range(0, count, chunk):
            hot = one_hot(wanted, first, (slots, chunk), 1)
            total += jnp.dot(
                hot, table_ref[t, pl.ds(first, chunk), :], preferred_element_type=jnp.float32
            )
        return total

    def table_step(t):
        got[t, me] = send_ref[t, me]
        for hop in range(1, n):
            deal(t, hop).wait_recv()
        grads = got[t].reshape(slots, width).astype(jnp.float32)
        rows = rows_ref[t]
        cols = [jnp.broadcast_to(rows[i : i + 1, :], (width, slots)).T[:, 0:1] for i in range(2)]
        quot_pick = pick(cols[0], slab_ref, t, quot_rows)
        for_rem = (grads * quot_pick).astype(jnp.bfloat16)
        chunk = max(share, 512)
        for first in range(0, rem_rows, chunk):
            hot = one_hot(rows[1:2, :], first, (chunk, slots), 0)
            grad = jnp.dot(hot, for_rem, preferred_element_type=jnp.float32)
            for r in range(first // share, (first + chunk) // share):
                where = tuple((r >> b) & 1 for b in range(levels - 1, -1, -1))
                part[(t,) + where] = grad[r * share - first : (r + 1) * share - first].astype(
                    jnp.bfloat16
                )
        halve(t, 0).start()
        rem_pick = pick(cols[1], rem_ref, t, rem_rows)
        for_quot = (grads * rem_pick).astype(jnp.bfloat16)
        chunk = min(quot_rows, 512)
        for first in range(0, quot_rows, chunk):
            here = pl.ds(first, chunk)
            hot = one_hot(rows[0:1, :], first, (chunk, slots), 0)
            grad = jnp.dot(hot, for_quot, preferred_element_type=jnp.float32)
            fresh, fresh_acc = adagrad(slab_ref[t, here, :], qacc_ref[t, :, here], grad)
            quot_ref[t, here, :] = fresh
            qacc_out_ref[t, :, here] = fresh_acc

    def adagrad(old, accum, grad):
        count = old.shape[0]
        mean = jnp.mean(grad * grad, axis=-1, keepdims=True)
        fresh_acc = jnp.broadcast_to(accum, (width, count)).T + mean
        fresh = old.astype(jnp.float32) - step_rate * grad * lax.rsqrt(fresh_acc + epsilon)
        return fresh.astype(jnp.bfloat16), fresh_acc.T[0:1, :]

    def sum_of(t, b, where):
        kept = stages[b][(t,) + where + (bits[b],)].astype(jnp.float32)
        return kept + landed[b][(t,) + where].astype(jnp.float32)

    def comm_step(t, s):
        if s <= levels:
            halve(t, s - 1).wait_recv()
            if s < levels:
                for i in range(1 << (levels - s)):
                    where = tuple((i >> b) & 1 for b in range(levels - s - 1, -1, -1))
                    held[s - 1][(t,) + where] = sum_of(t, s - 1, where).astype(jnp.bfloat16)
                halve(t, s).start()
            else:
                mine = pl.ds(pl.multiple_of(me * share, share), share)
                accum = racc_ref[t, :, mine]
                fresh, fresh_acc = adagrad(rem_ref[t, mine, :], accum, sum_of(t, s - 1, ()))
                rem_out_ref[(t,) + tuple(bits[::-1])] = fresh
                racc_out_ref[t] = fresh_acc
                spread(t, levels - 1).start()
        else:
            b = 2 * levels - s
            spread(t, b).wait_recv()
            if b > 0:
                spread(t, b - 1).start()

    def step(i, carry):
        @pl.when(i < tables)
        def _():
            table_step(i)

        for s in range(2 * levels, 0, -1):
            t = i - s

            @pl.when((t >= 0) & (t < tables))
            def _():
                comm_step(t, s)

        return carry

    lax.fori_loop(0, tables + 2 * levels, step, 0)

    def finish(t, carry):
        for hop in range(1, n):
            deal(t, hop).wait_send()
        for b in range(levels):
            halve(t, b).wait_send()
            spread(t, b).wait_send()
        return carry

    lax.fori_loop(0, tables, finish, 0)


def tables_call(send_rows, keys, slab, qacc, rem_table, rem_accum):
    tables, n, capacity, width = send_rows.shape
    levels = n.bit_length() - 1
    rem_rows, quot_rows = rem_table.shape[1], slab.shape[1]
    share = rem_rows // n
    both = jnp.stack((keys // rem_rows, keys % rem_rows), axis=1)
    vmem = pl.BlockSpec(memory_space=pltpu.VMEM)
    cube = lambda b: (tables,) + (2,) * b + (share, width)
    outs = pl.pallas_call(
        functools.partial(tables_kernel, n, levels),
        out_shape=(
            jax.ShapeDtypeStruct(slab.shape, jnp.bfloat16),
            jax.ShapeDtypeStruct((tables, 1, quot_rows), jnp.float32),
            jax.ShapeDtypeStruct(cube(levels), jnp.bfloat16),
            jax.ShapeDtypeStruct((tables, 1, share), jnp.float32),
        ),
        in_specs=[vmem] * 6,
        out_specs=(vmem,) * 4,
        scratch_shapes=[pltpu.VMEM((tables, n, capacity, width), jnp.bfloat16)]
        + [pltpu.VMEM(cube(b), jnp.bfloat16) for b in range(levels, 0, -1)]
        + [pltpu.VMEM(cube(b), jnp.bfloat16) for b in range(levels - 1, -1, -1)]
        + [pltpu.SemaphoreType.DMA((tables, n - 1))] * 2
        + [pltpu.SemaphoreType.DMA((2 * levels, tables))] * 2,
        compiler_params=pltpu.CompilerParams(
            collective_id=0, has_side_effects=True, vmem_limit_bytes=60 << 20
        ),
    )(
        send_rows,
        both,
        slab,
        qacc[:, None, :],
        rem_table,
        rem_accum[:, None, :],
    )
    quot_out, quot_acc_out, rem_out, rem_acc_out = outs
    return (
        quot_out,
        quot_acc_out[:, 0],
        rem_out.reshape(rem_table.shape),
        rem_acc_out[:, 0],
    )


def rank_kernel(
    n_row,
    n,
    levels,
    feats_ref,
    cotan_ref,
    in_ref,
    out_ref,
    bias_ref,
    keys_ref,
    pooled_ref,
    got_ref,
    part,
    full,
    *rest,
):
    held = list(rest[: levels - 1])
    landed = list(rest[levels - 1 : 2 * levels - 1])
    deal_send, deal_recv, send_sem, recv_sem = rest[2 * levels - 1 :]
    row = lax.axis_index("row")
    me = lax.axis_index("table")
    bits = digits(me, levels)
    every = slice(None)
    stages = [part] + held
    samples = feats_ref.shape[0]
    rank = in_ref.shape[1]
    share = samples // n

    def deal(hop):
        return pltpu.make_async_remote_copy(
            src_ref=keys_ref.at[lax.rem(row + hop, n_row)],
            dst_ref=got_ref.at[row],
            send_sem=deal_send.at[hop - 1],
            recv_sem=deal_recv.at[hop - 1],
            device_id={"row": lax.rem(row + hop, n_row)},
            device_id_type=MESH,
        )

    def halve(t, b):
        where = (t,) + (every,) * (levels - b - 1) + (1 - bits[b],)
        return pltpu.make_async_remote_copy(
            src_ref=stages[b].at[where],
            dst_ref=landed[b].at[t],
            send_sem=send_sem.at[b, t],
            recv_sem=recv_sem.at[b, t],
            device_id={"table": across(me, bits[b], b)},
            device_id_type=MESH,
        )

    def spread(t, b):
        where = (t,) + (every,) * (levels - b - 1) + tuple(bits[c] for c in range(b, -1, -1))
        return pltpu.make_async_remote_copy(
            src_ref=full.at[where],
            dst_ref=full.at[where],
            send_sem=send_sem.at[levels + b, t],
            recv_sem=recv_sem.at[levels + b, t],
            device_id={"table": across(me, bits[b], b)},
            device_id_type=MESH,
        )

    barrier = pltpu.get_barrier_semaphore()
    for axis, size, at in (("table", n, me), ("row", n_row, row)):
        for hop in range(1, size):
            pl.semaphore_signal(
                barrier, inc=1, device_id={axis: lax.rem(at + hop, size)}, device_id_type=MESH
            )
    pl.semaphore_wait(barrier, n + n_row - 2)
    for hop in range(1, n_row):
        deal(hop).start()

    def project(t, source, weight_ref):
        partial = jnp.dot(source, weight_ref[...], preferred_element_type=jnp.float32)
        part[t] = partial.astype(jnp.bfloat16).reshape(part.shape[1:])
        halve(t, 0).start()

    feats = feats_ref[...]
    cotan = cotan_ref[...].astype(jnp.float32)
    project(0, feats, in_ref)
    project(1, (cotan * feats.astype(jnp.float32)).astype(jnp.bfloat16), out_ref)
    got_ref[row] = keys_ref[row]
    for b in range(levels):
        for t in range(2):
            halve(t, b).wait_recv()
            mine = stages[b][(t,) + (every,) * (levels - b - 1) + (bits[b],)].astype(jnp.float32)
            total = (mine + landed[b][t].astype(jnp.float32)).astype(jnp.bfloat16)
            if b < levels - 1:
                held[b][t] = total
                halve(t, b + 1).start()
            else:
                full[(t,) + tuple(bits[::-1])] = total
                spread(t, b).start()
    for b in range(levels - 1, 0, -1):
        for t in range(2):
            spread(t, b).wait_recv()
            spread(t, b - 1).start()
    contract = (((1,), (1,)), ((), ()))
    back = []
    for t, weight_ref in ((0, out_ref), (1, in_ref)):
        spread(t, 0).wait_recv()
        whole = full[t].reshape(samples, rank)
        back.append(
            lax.dot_general(whole, weight_ref[...], contract, preferred_element_type=jnp.float32)
        )
    pooled = cotan * (back[0] + bias_ref[...] + 1.0) + back[1]
    pooled_ref[...] = pooled.astype(jnp.bfloat16)
    for hop in range(1, n_row):
        deal(hop).wait()
    for t in range(2):
        for b in range(levels):
            halve(t, b).wait_send()
            spread(t, b).wait_send()


def rank_call(features, cotangent, cross_in, cross_out, bias, keys):
    n_row, n = lax.axis_size("row"), lax.axis_size("table")
    levels = n.bit_length() - 1
    samples, columns = features.shape
    share, rank = samples // n, cross_in.shape[1]
    vmem = pl.BlockSpec(memory_space=pltpu.VMEM)
    cube = lambda b: pltpu.VMEM((2,) + (2,) * b + (share, rank), jnp.bfloat16)
    return pl.pallas_call(
        functools.partial(rank_kernel, n_row, n, levels),
        out_shape=(
            jax.ShapeDtypeStruct((samples, columns), jnp.bfloat16),
            jax.ShapeDtypeStruct(keys.shape, jnp.int32),
        ),
        in_specs=[vmem] * 6,
        out_specs=(vmem,) * 2,
        scratch_shapes=[cube(levels), cube(levels)]
        + [cube(b) for b in range(levels - 1, 0, -1)]
        + [cube(b) for b in range(levels - 1, -1, -1)]
        + [pltpu.SemaphoreType.DMA((n_row - 1,))] * 2
        + [pltpu.SemaphoreType.DMA((2 * levels, 2))] * 2,
        compiler_params=pltpu.CompilerParams(
            collective_id=1, has_side_effects=True, vmem_limit_bytes=60 << 20
        ),
    )(features, cotangent, cross_in, cross_out, bias[None, :], keys)


def per_device(
    features,
    cotangent,
    cross_in,
    cross_out,
    bias,
    dest_shard,
    quot_row,
    rem_row,
    quot_slab,
    quot_accum,
    rem_table,
    rem_accum,
):
    samples = features.shape[0]
    tables_dev = quot_slab.shape[0]
    row_width = quot_slab.shape[2]
    rem_rows = rem_table.shape[1]
    row_count = lax.axis_size("row")
    capacity = 3 * samples // (2 * row_count)
    slots = row_count * capacity
    target = dest_shard[:, :, 0]
    onehot = target[:, :, None] == jnp.arange(row_count, dtype=jnp.int32)[None, None, :]
    lower = (
        jnp.arange(samples, dtype=jnp.int32)[:, None]
        >= jnp.arange(samples, dtype=jnp.int32)[None, :]
    ).astype(jnp.bfloat16)
    running = jnp.einsum(
        "ij,tjn->tin", lower, onehot.astype(jnp.bfloat16), preferred_element_type=jnp.float32
    )
    slot_index = jnp.sum(jnp.where(onehot, running, 0.0), axis=2).astype(jnp.int32) - 1
    position = target * capacity + slot_index
    placed = position[:, :, None] == jnp.arange(slots, dtype=jnp.int32)[None, None, :]
    key_words = quot_row * rem_rows + rem_row
    send_keys = jnp.sum(jnp.where(placed, key_words[:, :, None], 0), axis=1)
    send_keys = send_keys.reshape(tables_dev, row_count, capacity).transpose(1, 0, 2)
    pooled, got_keys = rank_call(features, cotangent, cross_in, cross_out, bias, send_keys)
    pooled = pooled.reshape(samples, tables_dev, row_width)
    send_rows = jnp.einsum(
        "tsk,ste->tke", placed.astype(jnp.bfloat16), pooled, preferred_element_type=jnp.float32
    ).astype(jnp.bfloat16)
    send_rows = send_rows.reshape(tables_dev, row_count, capacity, row_width)
    got_keys = got_keys.transpose(1, 0, 2).reshape(tables_dev, slots)
    return tables_call(send_rows, got_keys, quot_slab, quot_accum, rem_table, rem_accum)


def solution(mesh):
    placed = (
        P("row", "table"),
        P("row", "table"),
        P("table", None),
        P("table", None),
        P("table"),
        P("table", "row", None),
        P("table", "row"),
        P("table", "row"),
        P("table", "row", None),
        P("table", "row"),
        P("table", None, None),
        P("table", None),
    )
    return jax.shard_map(
        per_device,
        mesh=mesh,
        in_specs=placed,
        out_specs=(
            P("table", "row", None),
            P("table", "row"),
            P("table", None, None),
            P("table", "row"),
        ),
        check_vma=False,
    )
```

```python
import functools

import jax
import jax.numpy as jnp
from jax import lax
from jax.experimental import pallas as pl
from jax.experimental.pallas import tpu as pltpu
from jax.sharding import PartitionSpec as P

step_rate = 0.3
epsilon = 1e-06
MESH = pl.DeviceIdType.MESH


def enter(axis, size):
    me = lax.axis_index(axis)
    barrier = pltpu.get_barrier_semaphore()
    for hop in range(1, size):
        pl.semaphore_signal(
            barrier, inc=1, device_id={axis: lax.rem(me + hop, size)}, device_id_type=MESH
        )
    pl.semaphore_wait(barrier, size - 1)


def digits(me, levels):
    return [lax.rem(me // (1 << b), 2) for b in range(levels)]


def across(me, bit, b):
    return me + (1 - 2 * bit) * (1 << b)


def one_hot(wanted, first, shape, axis):
    names = lax.broadcasted_iota(jnp.int32, shape, axis) + first
    return jnp.where(names == wanted, 1.0, 0.0).astype(jnp.bfloat16)


def tables_kernel(
    n,
    levels,
    send_ref,
    rows_ref,
    slab_ref,
    qacc_ref,
    rem_ref,
    racc_ref,
    quot_ref,
    qacc_out_ref,
    rem_out_ref,
    racc_out_ref,
    got,
    rem_keys,
    products,
    *rest,
):
    held = list(rest[: levels - 1])
    landed = list(rest[levels - 1 : 2 * levels - 2])
    key_send, key_recv, deal_send, deal_recv, send_sem, recv_sem = rest[2 * levels - 2 :]
    me = lax.axis_index("row")
    bits = digits(me, levels)
    tables, _, capacity, width = send_ref.shape
    slots = n * capacity
    rem_rows = rem_ref.shape[1]
    quot_rows = slab_ref.shape[1]
    share = rem_rows // n
    every = slice(None)
    down = list(range(levels - 1, -1, -1))
    orders = (tuple(down), tuple(down[:-2] + [0, 1]))

    def deal(t, hop):
        return pltpu.make_async_remote_copy(
            src_ref=send_ref.at[t, lax.rem(me + hop, n)],
            dst_ref=got.at[t, me],
            send_sem=deal_send.at[t, hop - 1],
            recv_sem=deal_recv.at[t, hop - 1],
            device_id={"row": lax.rem(me + hop, n)},
            device_id_type=MESH,
        )

    def swap_keys():
        return pltpu.make_async_remote_copy(
            src_ref=rem_keys.at[bits[0]],
            dst_ref=rem_keys.at[bits[0]],
            send_sem=key_send,
            recv_sem=key_recv,
            device_id={"row": across(me, bits[0], 0)},
            device_id_type=MESH,
        )

    def swap(t):
        return pltpu.make_async_remote_copy(
            src_ref=products.at[t, bits[0]],
            dst_ref=products.at[t, bits[0]],
            send_sem=send_sem.at[0, t],
            recv_sem=recv_sem.at[0, t],
            device_id={"row": across(me, bits[0], 0)},
            device_id_type=MESH,
        )

    def halve(t, b):
        where = (t,) + (every,) * (levels - b - 1) + (1 - bits[b],)
        return pltpu.make_async_remote_copy(
            src_ref=held[b - 1].at[where],
            dst_ref=landed[b - 1].at[t],
            send_sem=send_sem.at[b, t],
            recv_sem=recv_sem.at[b, t],
            device_id={"row": across(me, bits[b], b)},
            device_id_type=MESH,
        )

    def spread(t, j, order):
        done, b = order[:j], order[j]
        where = (t,) + tuple(every if c in done else bits[c] for c in down)
        return pltpu.make_async_remote_copy(
            src_ref=rem_out_ref.at[where],
            dst_ref=rem_out_ref.at[where],
            send_sem=send_sem.at[levels + j, t],
            recv_sem=recv_sem.at[levels + j, t],
            device_id={"row": across(me, bits[b], b)},
            device_id_type=MESH,
        )

    def by_order(t, act):
        last = lax.rem(t, 4) == 3
        for order, chosen in zip(orders, (jnp.logical_not(last), last)):

            @pl.when(chosen)
            def _():
                act(order)

    enter("row", n)

    def start_deal(t, carry):
        for hop in range(1, n):
            deal(t, hop).start()
        return carry

    lax.fori_loop(0, tables, start_deal, 0)
    rem_keys[bits[0]] = rows_ref[:, 1:2, :]
    swap_keys().start()

    def pick(wanted, table_ref, t, count):
        total = jnp.zeros((slots, width), jnp.float32)
        chunk = min(count, 512)
        for first in range(0, count, chunk):
            hot = one_hot(wanted, first, (slots, chunk), 1)
            total += jnp.dot(
                hot, table_ref[t, pl.ds(first, chunk), :], preferred_element_type=jnp.float32
            )
        return total

    def table_step(t):
        got[t, me] = send_ref[t, me]
        for hop in range(1, n):
            deal(t, hop).wait_recv()
        grads = got[t].reshape(slots, width).astype(jnp.float32)
        rows = rows_ref[t]
        cols = [jnp.broadcast_to(rows[i : i + 1, :], (width, slots)).T[:, 0:1] for i in range(2)]
        quot_pick = pick(cols[0], slab_ref, t, quot_rows)
        for_rem = (grads * quot_pick).astype(jnp.bfloat16)
        products[t, bits[0]] = for_rem
        swap(t).start()
        rem_pick = pick(cols[1], rem_ref, t, rem_rows)
        for_quot = (grads * rem_pick).astype(jnp.bfloat16)
        chunk = min(quot_rows, 512)
        for first in range(0, quot_rows, chunk):
            here = pl.ds(first, chunk)
            hot = one_hot(rows[0:1, :], first, (chunk, slots), 0)
            grad = jnp.dot(hot, for_quot, preferred_element_type=jnp.float32)
            fresh, fresh_acc = adagrad(slab_ref[t, here, :], qacc_ref[t, :, here], grad)
            quot_ref[t, here, :] = fresh
            qacc_out_ref[t, :, here] = fresh_acc

    def adagrad(old, accum, grad):
        count = old.shape[0]
        mean = jnp.mean(grad * grad, axis=-1, keepdims=True)
        fresh_acc = jnp.broadcast_to(accum, (width, count)).T + mean
        fresh = old.astype(jnp.float32) - step_rate * grad * lax.rsqrt(fresh_acc + epsilon)
        return fresh.astype(jnp.bfloat16), fresh_acc.T[0:1, :]

    def sum_of(t, b, where):
        kept = held[b - 1][(t,) + where + (bits[b],)].astype(jnp.float32)
        return kept + landed[b - 1][(t,) + where].astype(jnp.float32)

    def half_grad(t):
        for j in range(0, n // 2, 2):
            near = lax.broadcasted_iota(jnp.int32, (2 * share, slots), 0)
            names = near + jnp.where(near >= share, share, 0) + (2 * j + bits[0]) * share
            grad = jnp.zeros((2 * share, width), jnp.float32)
            for side in range(2):
                hot = jnp.where(names == rem_keys[side, t], 1.0, 0.0).astype(jnp.bfloat16)
                grad += jnp.dot(hot, products[t, side], preferred_element_type=jnp.float32)
            for i in range(2):
                where = tuple(((j + i) >> b) & 1 for b in range(levels - 2, -1, -1))
                held[0][(t,) + where] = grad[i * share : (i + 1) * share].astype(jnp.bfloat16)

    def comm_step(t, s):
        if s == 1:
            pl.when(t == 0)(lambda: swap_keys().wait_recv())
            swap(t).wait_recv()
            half_grad(t)
            halve(t, 1).start()
        elif s <= levels:
            halve(t, s - 1).wait_recv()
            if s < levels:
                for i in range(1 << (levels - s)):
                    where = tuple((i >> b) & 1 for b in range(levels - s - 1, -1, -1))
                    held[s - 1][(t,) + where] = sum_of(t, s - 1, where).astype(jnp.bfloat16)
                halve(t, s).start()
            else:
                mine = pl.ds(pl.multiple_of(me * share, share), share)
                accum = racc_ref[t, :, mine]
                fresh, fresh_acc = adagrad(rem_ref[t, mine, :], accum, sum_of(t, s - 1, ()))
                rem_out_ref[(t,) + tuple(bits[::-1])] = fresh
                racc_out_ref[t] = fresh_acc
                by_order(t, lambda order: spread(t, 0, order).start())
        else:
            j = s - levels - 1

            def pass_on(order):
                spread(t, j, order).wait_recv()
                if j < levels - 1:
                    spread(t, j + 1, order).start()

            by_order(t, pass_on)

    def step(i, carry):
        @pl.when(i < tables)
        def _():
            table_step(i)

        for s in range(2 * levels, 0, -1):
            t = i - s

            @pl.when((t >= 0) & (t < tables))
            def _():
                comm_step(t, s)

        return carry

    lax.fori_loop(0, tables + 2 * levels, step, 0)

    def finish(t, carry):
        for hop in range(1, n):
            deal(t, hop).wait_send()
        swap(t).wait_send()
        for b in range(1, levels):
            halve(t, b).wait_send()

        def sent(order):
            for j in range(levels):
                spread(t, j, order).wait_send()

        by_order(t, sent)
        return carry

    lax.fori_loop(0, tables, finish, 0)
    swap_keys().wait_send()


def tables_call(send_rows, keys, slab, qacc, rem_table, rem_accum):
    tables, n, capacity, width = send_rows.shape
    levels = n.bit_length() - 1
    rem_rows, quot_rows = rem_table.shape[1], slab.shape[1]
    share = rem_rows // n
    both = jnp.stack((keys // rem_rows, keys % rem_rows), axis=1)
    vmem = pl.BlockSpec(memory_space=pltpu.VMEM)
    cube = lambda b: (tables,) + (2,) * b + (share, width)
    outs = pl.pallas_call(
        functools.partial(tables_kernel, n, levels),
        out_shape=(
            jax.ShapeDtypeStruct(slab.shape, jnp.bfloat16),
            jax.ShapeDtypeStruct((tables, 1, quot_rows), jnp.float32),
            jax.ShapeDtypeStruct(cube(levels), jnp.bfloat16),
            jax.ShapeDtypeStruct((tables, 1, share), jnp.float32),
        ),
        in_specs=[vmem] * 6,
        out_specs=(vmem,) * 4,
        scratch_shapes=[pltpu.VMEM((tables, n, capacity, width), jnp.bfloat16)]
        + [
            pltpu.VMEM((2, tables, 1, n * capacity), jnp.int32),
            pltpu.VMEM((tables, 2, n * capacity, width), jnp.bfloat16),
        ]
        + [pltpu.VMEM(cube(b), jnp.bfloat16) for b in range(levels - 1, 0, -1)]
        + [pltpu.VMEM(cube(b), jnp.bfloat16) for b in range(levels - 2, -1, -1)]
        + [pltpu.SemaphoreType.DMA(())] * 2
        + [pltpu.SemaphoreType.DMA((tables, n - 1))] * 2
        + [pltpu.SemaphoreType.DMA((2 * levels, tables))] * 2,
        compiler_params=pltpu.CompilerParams(
            collective_id=0, has_side_effects=True, vmem_limit_bytes=60 << 20
        ),
    )(
        send_rows,
        both,
        slab,
        qacc[:, None, :],
        rem_table,
        rem_accum[:, None, :],
    )
    quot_out, quot_acc_out, rem_out, rem_acc_out = outs
    return (
        quot_out,
        quot_acc_out[:, 0],
        rem_out.reshape(rem_table.shape),
        rem_acc_out[:, 0],
    )


def rank_kernel(
    n_row,
    n,
    levels,
    feats_ref,
    cotan_ref,
    in_ref,
    out_ref,
    bias_ref,
    keys_ref,
    pooled_ref,
    got_ref,
    part,
    full,
    *rest,
):
    held = list(rest[: levels - 1])
    landed = list(rest[levels - 1 : 2 * levels - 1])
    deal_send, deal_recv, send_sem, recv_sem = rest[2 * levels - 1 :]
    row = lax.axis_index("row")
    me = lax.axis_index("table")
    bits = digits(me, levels)
    every = slice(None)
    stages = [part] + held
    samples = feats_ref.shape[0]
    rank = in_ref.shape[1]
    share = samples // n

    def deal(hop):
        return pltpu.make_async_remote_copy(
            src_ref=keys_ref.at[lax.rem(row + hop, n_row)],
            dst_ref=got_ref.at[row],
            send_sem=deal_send.at[hop - 1],
            recv_sem=deal_recv.at[hop - 1],
            device_id={"row": lax.rem(row + hop, n_row)},
            device_id_type=MESH,
        )

    def halve(t, b):
        where = (t,) + (every,) * (levels - b - 1) + (1 - bits[b],)
        return pltpu.make_async_remote_copy(
            src_ref=stages[b].at[where],
            dst_ref=landed[b].at[t],
            send_sem=send_sem.at[b, t],
            recv_sem=recv_sem.at[b, t],
            device_id={"table": across(me, bits[b], b)},
            device_id_type=MESH,
        )

    def spread(t, b):
        where = (t,) + (every,) * (levels - b - 1) + tuple(bits[c] for c in range(b, -1, -1))
        return pltpu.make_async_remote_copy(
            src_ref=full.at[where],
            dst_ref=full.at[where],
            send_sem=send_sem.at[levels + b, t],
            recv_sem=recv_sem.at[levels + b, t],
            device_id={"table": across(me, bits[b], b)},
            device_id_type=MESH,
        )

    barrier = pltpu.get_barrier_semaphore()
    for axis, size, at in (("table", n, me), ("row", n_row, row)):
        for hop in range(1, size):
            pl.semaphore_signal(
                barrier, inc=1, device_id={axis: lax.rem(at + hop, size)}, device_id_type=MESH
            )
    pl.semaphore_wait(barrier, n + n_row - 2)
    for hop in range(1, n_row):
        deal(hop).start()

    def project(t, source, weight_ref):
        partial = jnp.dot(source, weight_ref[...], preferred_element_type=jnp.float32)
        part[t] = partial.astype(jnp.bfloat16).reshape(part.shape[1:])
        halve(t, 0).start()

    feats = feats_ref[...]
    cotan = cotan_ref[...].astype(jnp.float32)
    project(0, feats, in_ref)
    project(1, (cotan * feats.astype(jnp.float32)).astype(jnp.bfloat16), out_ref)
    got_ref[row] = keys_ref[row]
    for b in range(levels):
        for t in range(2):
            halve(t, b).wait_recv()
            mine = stages[b][(t,) + (every,) * (levels - b - 1) + (bits[b],)].astype(jnp.float32)
            total = (mine + landed[b][t].astype(jnp.float32)).astype(jnp.bfloat16)
            if b < levels - 1:
                held[b][t] = total
                halve(t, b + 1).start()
            else:
                full[(t,) + tuple(bits[::-1])] = total
                spread(t, b).start()
    for b in range(levels - 1, 0, -1):
        for t in range(2):
            spread(t, b).wait_recv()
            spread(t, b - 1).start()
    contract = (((1,), (1,)), ((), ()))
    back = []
    for t, weight_ref in ((0, out_ref), (1, in_ref)):
        spread(t, 0).wait_recv()
        whole = full[t].reshape(samples, rank)
        back.append(
            lax.dot_general(whole, weight_ref[...], contract, preferred_element_type=jnp.float32)
        )
    pooled = cotan * (back[0] + bias_ref[...] + 1.0) + back[1]
    pooled_ref[...] = pooled.astype(jnp.bfloat16)
    for hop in range(1, n_row):
        deal(hop).wait()
    for t in range(2):
        for b in range(levels):
            halve(t, b).wait_send()
            spread(t, b).wait_send()


def rank_call(features, cotangent, cross_in, cross_out, bias, keys):
    n_row, n = lax.axis_size("row"), lax.axis_size("table")
    levels = n.bit_length() - 1
    samples, columns = features.shape
    share, rank = samples // n, cross_in.shape[1]
    vmem = pl.BlockSpec(memory_space=pltpu.VMEM)
    cube = lambda b: pltpu.VMEM((2,) + (2,) * b + (share, rank), jnp.bfloat16)
    return pl.pallas_call(
        functools.partial(rank_kernel, n_row, n, levels),
        out_shape=(
            jax.ShapeDtypeStruct((samples, columns), jnp.bfloat16),
            jax.ShapeDtypeStruct(keys.shape, jnp.int32),
        ),
        in_specs=[vmem] * 6,
        out_specs=(vmem,) * 2,
        scratch_shapes=[cube(levels), cube(levels)]
        + [cube(b) for b in range(levels - 1, 0, -1)]
        + [cube(b) for b in range(levels - 1, -1, -1)]
        + [pltpu.SemaphoreType.DMA((n_row - 1,))] * 2
        + [pltpu.SemaphoreType.DMA((2 * levels, 2))] * 2,
        compiler_params=pltpu.CompilerParams(
            collective_id=1, has_side_effects=True, vmem_limit_bytes=60 << 20
        ),
    )(features, cotangent, cross_in, cross_out, bias[None, :], keys)


def per_device(
    features,
    cotangent,
    cross_in,
    cross_out,
    bias,
    dest_shard,
    quot_row,
    rem_row,
    quot_slab,
    quot_accum,
    rem_table,
    rem_accum,
):
    samples = features.shape[0]
    tables_dev = quot_slab.shape[0]
    row_width = quot_slab.shape[2]
    rem_rows = rem_table.shape[1]
    row_count = lax.axis_size("row")
    capacity = 3 * samples // (2 * row_count)
    slots = row_count * capacity
    target = dest_shard[:, :, 0]
    onehot = target[:, :, None] == jnp.arange(row_count, dtype=jnp.int32)[None, None, :]
    lower = (
        jnp.arange(samples, dtype=jnp.int32)[:, None]
        >= jnp.arange(samples, dtype=jnp.int32)[None, :]
    ).astype(jnp.bfloat16)
    running = jnp.einsum(
        "ij,tjn->tin", lower, onehot.astype(jnp.bfloat16), preferred_element_type=jnp.float32
    )
    slot_index = jnp.sum(jnp.where(onehot, running, 0.0), axis=2).astype(jnp.int32) - 1
    position = target * capacity + slot_index
    placed = position[:, :, None] == jnp.arange(slots, dtype=jnp.int32)[None, None, :]
    key_words = quot_row * rem_rows + rem_row
    send_keys = jnp.sum(jnp.where(placed, key_words[:, :, None], 0), axis=1)
    send_keys = send_keys.reshape(tables_dev, row_count, capacity).transpose(1, 0, 2)
    pooled, got_keys = rank_call(features, cotangent, cross_in, cross_out, bias, send_keys)
    pooled = pooled.reshape(samples, tables_dev, row_width)
    send_rows = jnp.einsum(
        "tsk,ste->tke", placed.astype(jnp.bfloat16), pooled, preferred_element_type=jnp.float32
    ).astype(jnp.bfloat16)
    send_rows = send_rows.reshape(tables_dev, row_count, capacity, row_width)
    got_keys = got_keys.transpose(1, 0, 2).reshape(tables_dev, slots)
    return tables_call(send_rows, got_keys, quot_slab, quot_accum, rem_table, rem_accum)


def solution(mesh):
    placed = (
        P("row", "table"),
        P("row", "table"),
        P("table", None),
        P("table", None),
        P("table"),
        P("table", "row", None),
        P("table", "row"),
        P("table", "row"),
        P("table", "row", None),
        P("table", "row"),
        P("table", None, None),
        P("table", None),
    )
    return jax.shard_map(
        per_device,
        mesh=mesh,
        in_specs=placed,
        out_specs=(
            P("table", "row", None),
            P("table", "row"),
            P("table", None, None),
            P("table", "row"),
        ),
        check_vma=False,
    )
```

```python
import functools

import jax
import jax.numpy as jnp
from jax import lax
from jax.experimental import pallas as pl
from jax.experimental.pallas import tpu as pltpu
from jax.sharding import PartitionSpec as P

step_rate = 0.3
epsilon = 1e-06
MESH = pl.DeviceIdType.MESH


def enter(axis, size):
    me = lax.axis_index(axis)
    barrier = pltpu.get_barrier_semaphore()
    for hop in range(1, size):
        pl.semaphore_signal(
            barrier, inc=1, device_id={axis: lax.rem(me + hop, size)}, device_id_type=MESH
        )
    pl.semaphore_wait(barrier, size - 1)


def digits(me, levels):
    return [lax.rem(me // (1 << b), 2) for b in range(levels)]


def across(me, bit, b):
    return me + (1 - 2 * bit) * (1 << b)


def one_hot(wanted, first, shape, axis):
    small = lambda x: x.astype(jnp.float32).astype(jnp.bfloat16)
    size = min(shape[axis], 256)
    part = shape[:axis] + (size,) + shape[axis + 1 :]
    names = small(lax.broadcasted_iota(jnp.int32, part, axis))
    one, zero = jnp.ones(part, jnp.bfloat16), jnp.zeros(part, jnp.bfloat16)
    hots = []
    for start in range(first, first + shape[axis], size):
        local = wanted - start
        local = small(jnp.where((local >= 0) & (local < size), local, -1))
        hots.append(jnp.where(names == local, one, zero))
    return jnp.concatenate(hots, axis=axis)


def tables_kernel(
    n,
    levels,
    send_ref,
    rows_ref,
    slab_ref,
    qacc_ref,
    rem_ref,
    racc_ref,
    quot_ref,
    qacc_out_ref,
    rem_out_ref,
    racc_out_ref,
    got,
    part,
    *rest,
):
    held = list(rest[: levels - 1])
    landed = list(rest[levels - 1 : 2 * levels - 1])
    deal_send, deal_recv, send_sem, recv_sem = rest[2 * levels - 1 :]
    me = lax.axis_index("row")
    bits = digits(me, levels)
    tables, _, capacity, width = send_ref.shape
    slots = n * capacity
    rem_rows = rem_ref.shape[1]
    quot_rows = slab_ref.shape[1]
    share = rem_rows // n
    every = slice(None)
    stages = [part] + held

    def deal(t, hop):
        return pltpu.make_async_remote_copy(
            src_ref=send_ref.at[t, lax.rem(me + hop, n)],
            dst_ref=got.at[t, me],
            send_sem=deal_send.at[t, hop - 1],
            recv_sem=deal_recv.at[t, hop - 1],
            device_id={"row": lax.rem(me + hop, n)},
            device_id_type=MESH,
        )

    def halve(t, b):
        where = (t,) + (every,) * (levels - b - 1) + (1 - bits[b],)
        return pltpu.make_async_remote_copy(
            src_ref=stages[b].at[where],
            dst_ref=landed[b].at[t],
            send_sem=send_sem.at[b, t],
            recv_sem=recv_sem.at[b, t],
            device_id={"row": across(me, bits[b], b)},
            device_id_type=MESH,
        )

    def spread(t, b):
        where = (t,) + (every,) * (levels - b - 1) + tuple(bits[c] for c in range(b, -1, -1))
        return pltpu.make_async_remote_copy(
            src_ref=rem_out_ref.at[where],
            dst_ref=rem_out_ref.at[where],
            send_sem=send_sem.at[levels + b, t],
            recv_sem=recv_sem.at[levels + b, t],
            device_id={"row": across(me, bits[b], b)},
            device_id_type=MESH,
        )

    enter("row", n)

    def start_deal(t, carry):
        for hop in range(1, n):
            deal(t, hop).start()
        return carry

    lax.fori_loop(0, tables, start_deal, 0)

    def pick(wanted, table_ref, t, count):
        total = jnp.zeros((slots, width), jnp.float32)
        chunk = min(count, 512)
        for first in range(0, count, chunk):
            hot = one_hot(wanted, first, (slots, chunk), 1)
            total += jnp.dot(
                hot, table_ref[t, pl.ds(first, chunk), :], preferred_element_type=jnp.float32
            )
        return total

    def table_step(t):
        got[t, me] = send_ref[t, me]
        for hop in range(1, n):
            deal(t, hop).wait_recv()
        grads = got[t].reshape(slots, width).astype(jnp.float32)
        rows = rows_ref[t]
        cols = [jnp.broadcast_to(rows[i : i + 1, :], (width, slots)).T[:, 0:1] for i in range(2)]
        quot_pick = pick(cols[0], slab_ref, t, quot_rows)
        for_rem = (grads * quot_pick).astype(jnp.bfloat16)
        chunk = max(share, 512)
        for first in range(0, rem_rows, chunk):
            hot = one_hot(rows[1:2, :], first, (chunk, slots), 0)
            grad = jnp.dot(hot, for_rem, preferred_element_type=jnp.float32)
            for r in range(first // share, (first + chunk) // share):
                where = tuple((r >> b) & 1 for b in range(levels - 1, -1, -1))
                part[(t,) + where] = grad[r * share - first : (r + 1) * share - first].astype(
                    jnp.bfloat16
                )
        halve(t, 0).start()
        rem_pick = pick(cols[1], rem_ref, t, rem_rows)
        for_quot = (grads * rem_pick).astype(jnp.bfloat16)
        chunk = min(quot_rows, 512)
        for first in range(0, quot_rows, chunk):
            here = pl.ds(first, chunk)
            hot = one_hot(rows[0:1, :], first, (chunk, slots), 0)
            grad = jnp.dot(hot, for_quot, preferred_element_type=jnp.float32)
            fresh, fresh_acc = adagrad(slab_ref[t, here, :], qacc_ref[t, :, here], grad)
            quot_ref[t, here, :] = fresh
            qacc_out_ref[t, :, here] = fresh_acc

    def adagrad(old, accum, grad):
        count = old.shape[0]
        mean = jnp.mean(grad * grad, axis=-1, keepdims=True)
        fresh_acc = jnp.broadcast_to(accum, (width, count)).T + mean
        fresh = old.astype(jnp.float32) - step_rate * grad * lax.rsqrt(fresh_acc + epsilon)
        return fresh.astype(jnp.bfloat16), fresh_acc.T[0:1, :]

    def sum_of(t, b, where):
        kept = stages[b][(t,) + where + (bits[b],)].astype(jnp.float32)
        return kept + landed[b][(t,) + where].astype(jnp.float32)

    def comm_step(t, s):
        if s <= levels:
            halve(t, s - 1).wait_recv()
            if s < levels:
                for i in range(1 << (levels - s)):
                    where = tuple((i >> b) & 1 for b in range(levels - s - 1, -1, -1))
                    held[s - 1][(t,) + where] = sum_of(t, s - 1, where).astype(jnp.bfloat16)
                halve(t, s).start()
            else:
                mine = pl.ds(pl.multiple_of(me * share, share), share)
                accum = racc_ref[t, :, mine]
                fresh, fresh_acc = adagrad(rem_ref[t, mine, :], accum, sum_of(t, s - 1, ()))
                rem_out_ref[(t,) + tuple(bits[::-1])] = fresh
                racc_out_ref[t] = fresh_acc
                spread(t, levels - 1).start()
        else:
            b = 2 * levels - s
            spread(t, b).wait_recv()
            if b > 0:
                spread(t, b - 1).start()

    def step(i, carry):
        @pl.when(i < tables)
        def _():
            table_step(i)

        for s in range(2 * levels, 0, -1):
            t = i - s

            @pl.when((t >= 0) & (t < tables))
            def _():
                comm_step(t, s)

        return carry

    lax.fori_loop(0, tables + 2 * levels, step, 0)

    def finish(t, carry):
        for hop in range(1, n):
            deal(t, hop).wait_send()
        for b in range(levels):
            halve(t, b).wait_send()
            spread(t, b).wait_send()
        return carry

    lax.fori_loop(0, tables, finish, 0)


def tables_call(send_rows, keys, slab, qacc, rem_table, rem_accum):
    tables, n, capacity, width = send_rows.shape
    levels = n.bit_length() - 1
    rem_rows, quot_rows = rem_table.shape[1], slab.shape[1]
    share = rem_rows // n
    both = jnp.stack((keys // rem_rows, keys % rem_rows), axis=1)
    vmem = pl.BlockSpec(memory_space=pltpu.VMEM)
    cube = lambda b: (tables,) + (2,) * b + (share, width)
    outs = pl.pallas_call(
        functools.partial(tables_kernel, n, levels),
        out_shape=(
            jax.ShapeDtypeStruct(slab.shape, jnp.bfloat16),
            jax.ShapeDtypeStruct((tables, 1, quot_rows), jnp.float32),
            jax.ShapeDtypeStruct(cube(levels), jnp.bfloat16),
            jax.ShapeDtypeStruct((tables, 1, share), jnp.float32),
        ),
        in_specs=[vmem] * 6,
        out_specs=(vmem,) * 4,
        scratch_shapes=[pltpu.VMEM((tables, n, capacity, width), jnp.bfloat16)]
        + [pltpu.VMEM(cube(b), jnp.bfloat16) for b in range(levels, 0, -1)]
        + [pltpu.VMEM(cube(b), jnp.bfloat16) for b in range(levels - 1, -1, -1)]
        + [pltpu.SemaphoreType.DMA((tables, n - 1))] * 2
        + [pltpu.SemaphoreType.DMA((2 * levels, tables))] * 2,
        compiler_params=pltpu.CompilerParams(
            collective_id=0, has_side_effects=True, vmem_limit_bytes=60 << 20
        ),
    )(
        send_rows,
        both,
        slab,
        qacc[:, None, :],
        rem_table,
        rem_accum[:, None, :],
    )
    quot_out, quot_acc_out, rem_out, rem_acc_out = outs
    return (
        quot_out,
        quot_acc_out[:, 0],
        rem_out.reshape(rem_table.shape),
        rem_acc_out[:, 0],
    )


def rank_kernel(
    n_row,
    n,
    levels,
    feats_ref,
    cotan_ref,
    in_ref,
    out_ref,
    bias_ref,
    keys_ref,
    pooled_ref,
    got_ref,
    part,
    full,
    *rest,
):
    held = list(rest[: levels - 1])
    landed = list(rest[levels - 1 : 2 * levels - 1])
    deal_send, deal_recv, send_sem, recv_sem = rest[2 * levels - 1 :]
    row = lax.axis_index("row")
    me = lax.axis_index("table")
    bits = digits(me, levels)
    every = slice(None)
    stages = [part] + held
    samples = feats_ref.shape[0]
    rank = in_ref.shape[1]
    share = samples // n

    def deal(hop):
        return pltpu.make_async_remote_copy(
            src_ref=keys_ref.at[lax.rem(row + hop, n_row)],
            dst_ref=got_ref.at[row],
            send_sem=deal_send.at[hop - 1],
            recv_sem=deal_recv.at[hop - 1],
            device_id={"row": lax.rem(row + hop, n_row)},
            device_id_type=MESH,
        )

    def halve(t, b):
        where = (t,) + (every,) * (levels - b - 1) + (1 - bits[b],)
        return pltpu.make_async_remote_copy(
            src_ref=stages[b].at[where],
            dst_ref=landed[b].at[t],
            send_sem=send_sem.at[b, t],
            recv_sem=recv_sem.at[b, t],
            device_id={"table": across(me, bits[b], b)},
            device_id_type=MESH,
        )

    def spread(t, b):
        where = (t,) + (every,) * (levels - b - 1) + tuple(bits[c] for c in range(b, -1, -1))
        return pltpu.make_async_remote_copy(
            src_ref=full.at[where],
            dst_ref=full.at[where],
            send_sem=send_sem.at[levels + b, t],
            recv_sem=recv_sem.at[levels + b, t],
            device_id={"table": across(me, bits[b], b)},
            device_id_type=MESH,
        )

    barrier = pltpu.get_barrier_semaphore()
    for axis, size, at in (("table", n, me), ("row", n_row, row)):
        for hop in range(1, size):
            pl.semaphore_signal(
                barrier, inc=1, device_id={axis: lax.rem(at + hop, size)}, device_id_type=MESH
            )
    pl.semaphore_wait(barrier, n + n_row - 2)
    for hop in range(1, n_row):
        deal(hop).start()

    def project(t, source, weight_ref):
        partial = jnp.dot(source, weight_ref[...], preferred_element_type=jnp.float32)
        part[t] = partial.astype(jnp.bfloat16).reshape(part.shape[1:])
        halve(t, 0).start()

    feats = feats_ref[...]
    cotan = cotan_ref[...].astype(jnp.float32)
    project(0, feats, in_ref)
    project(1, (cotan * feats.astype(jnp.float32)).astype(jnp.bfloat16), out_ref)
    got_ref[row] = keys_ref[row]
    for b in range(levels):
        for t in range(2):
            halve(t, b).wait_recv()
            mine = stages[b][(t,) + (every,) * (levels - b - 1) + (bits[b],)].astype(jnp.float32)
            total = (mine + landed[b][t].astype(jnp.float32)).astype(jnp.bfloat16)
            if b < levels - 1:
                held[b][t] = total
                halve(t, b + 1).start()
            else:
                full[(t,) + tuple(bits[::-1])] = total
                spread(t, b).start()
    for b in range(levels - 1, 0, -1):
        for t in range(2):
            spread(t, b).wait_recv()
            spread(t, b - 1).start()
    contract = (((1,), (1,)), ((), ()))
    back = []
    for t, weight_ref in ((0, out_ref), (1, in_ref)):
        spread(t, 0).wait_recv()
        whole = full[t].reshape(samples, rank)
        back.append(
            lax.dot_general(whole, weight_ref[...], contract, preferred_element_type=jnp.float32)
        )
    pooled = cotan * (back[0] + bias_ref[...] + 1.0) + back[1]
    pooled_ref[...] = pooled.astype(jnp.bfloat16)
    for hop in range(1, n_row):
        deal(hop).wait()
    for t in range(2):
        for b in range(levels):
            halve(t, b).wait_send()
            spread(t, b).wait_send()


def rank_call(features, cotangent, cross_in, cross_out, bias, keys):
    n_row, n = lax.axis_size("row"), lax.axis_size("table")
    levels = n.bit_length() - 1
    samples, columns = features.shape
    share, rank = samples // n, cross_in.shape[1]
    vmem = pl.BlockSpec(memory_space=pltpu.VMEM)
    cube = lambda b: pltpu.VMEM((2,) + (2,) * b + (share, rank), jnp.bfloat16)
    return pl.pallas_call(
        functools.partial(rank_kernel, n_row, n, levels),
        out_shape=(
            jax.ShapeDtypeStruct((samples, columns), jnp.bfloat16),
            jax.ShapeDtypeStruct(keys.shape, jnp.int32),
        ),
        in_specs=[vmem] * 6,
        out_specs=(vmem,) * 2,
        scratch_shapes=[cube(levels), cube(levels)]
        + [cube(b) for b in range(levels - 1, 0, -1)]
        + [cube(b) for b in range(levels - 1, -1, -1)]
        + [pltpu.SemaphoreType.DMA((n_row - 1,))] * 2
        + [pltpu.SemaphoreType.DMA((2 * levels, 2))] * 2,
        compiler_params=pltpu.CompilerParams(
            collective_id=1, has_side_effects=True, vmem_limit_bytes=60 << 20
        ),
    )(features, cotangent, cross_in, cross_out, bias[None, :], keys)


def per_device(
    features,
    cotangent,
    cross_in,
    cross_out,
    bias,
    dest_shard,
    quot_row,
    rem_row,
    quot_slab,
    quot_accum,
    rem_table,
    rem_accum,
):
    samples = features.shape[0]
    tables_dev = quot_slab.shape[0]
    row_width = quot_slab.shape[2]
    rem_rows = rem_table.shape[1]
    row_count = lax.axis_size("row")
    capacity = 3 * samples // (2 * row_count)
    slots = row_count * capacity
    target = dest_shard[:, :, 0]
    onehot = target[:, :, None] == jnp.arange(row_count, dtype=jnp.int32)[None, None, :]
    lower = (
        jnp.arange(samples, dtype=jnp.int32)[:, None]
        >= jnp.arange(samples, dtype=jnp.int32)[None, :]
    ).astype(jnp.bfloat16)
    running = jnp.einsum(
        "ij,tjn->tin", lower, onehot.astype(jnp.bfloat16), preferred_element_type=jnp.float32
    )
    slot_index = jnp.sum(jnp.where(onehot, running, 0.0), axis=2).astype(jnp.int32) - 1
    position = target * capacity + slot_index
    placed = position[:, :, None] == jnp.arange(slots, dtype=jnp.int32)[None, None, :]
    key_words = quot_row * rem_rows + rem_row
    send_keys = jnp.sum(jnp.where(placed, key_words[:, :, None], 0), axis=1)
    send_keys = send_keys.reshape(tables_dev, row_count, capacity).transpose(1, 0, 2)
    pooled, got_keys = rank_call(features, cotangent, cross_in, cross_out, bias, send_keys)
    pooled = pooled.reshape(samples, tables_dev, row_width)
    send_rows = jnp.einsum(
        "tsk,ste->tke", placed.astype(jnp.bfloat16), pooled, preferred_element_type=jnp.float32
    ).astype(jnp.bfloat16)
    send_rows = send_rows.reshape(tables_dev, row_count, capacity, row_width)
    got_keys = got_keys.transpose(1, 0, 2).reshape(tables_dev, slots)
    return tables_call(send_rows, got_keys, quot_slab, quot_accum, rem_table, rem_accum)


def solution(mesh):
    placed = (
        P("row", "table"),
        P("row", "table"),
        P("table", None),
        P("table", None),
        P("table"),
        P("table", "row", None),
        P("table", "row"),
        P("table", "row"),
        P("table", "row", None),
        P("table", "row"),
        P("table", None, None),
        P("table", None),
    )
    return jax.shard_map(
        per_device,
        mesh=mesh,
        in_specs=placed,
        out_specs=(
            P("table", "row", None),
            P("table", "row"),
            P("table", None, None),
            P("table", "row"),
        ),
        check_vma=False,
    )
```

```python
import functools

import jax
import jax.numpy as jnp
from jax import lax
from jax.experimental import pallas as pl
from jax.experimental.pallas import tpu as pltpu
from jax.sharding import PartitionSpec as P

step_rate = 0.3
epsilon = 1e-06
MESH = pl.DeviceIdType.MESH


def enter(axis, size):
    me = lax.axis_index(axis)
    barrier = pltpu.get_barrier_semaphore()
    for hop in range(1, size):
        pl.semaphore_signal(
            barrier, inc=1, device_id={axis: lax.rem(me + hop, size)}, device_id_type=MESH
        )
    pl.semaphore_wait(barrier, size - 1)


def digits(me, levels):
    return [lax.rem(me // (1 << b), 2) for b in range(levels)]


def across(me, bit, b):
    return me + (1 - 2 * bit) * (1 << b)


def one_hot(wanted, first, shape, axis):
    small = lambda x: x.astype(jnp.float32).astype(jnp.bfloat16)
    size = min(shape[axis], 256)
    part = shape[:axis] + (size,) + shape[axis + 1 :]
    names = small(lax.broadcasted_iota(jnp.int32, part, axis))
    one, zero = jnp.ones(part, jnp.bfloat16), jnp.zeros(part, jnp.bfloat16)
    hots = []
    for start in range(0, shape[axis], size):
        local = wanted - (first + start)
        local = small(jnp.where((local >= 0) & (local < size), local, -1))
        hots.append(jnp.where(names == local, one, zero))
    return jnp.concatenate(hots, axis=axis)


def tables_kernel(
    n,
    levels,
    send_ref,
    rows_ref,
    slab_ref,
    qacc_ref,
    rem_ref,
    racc_ref,
    quot_ref,
    qacc_out_ref,
    rem_out_ref,
    racc_out_ref,
    got,
    rem_keys,
    products,
    *rest,
):
    held = list(rest[: levels - 1])
    landed = list(rest[levels - 1 : 2 * levels - 2])
    key_send, key_recv, deal_send, deal_recv, send_sem, recv_sem = rest[2 * levels - 2 :]
    me = lax.axis_index("row")
    bits = digits(me, levels)
    tables, _, capacity, width = send_ref.shape
    slots = n * capacity
    rem_rows = rem_ref.shape[1]
    quot_rows = slab_ref.shape[1]
    share = rem_rows // n
    every = slice(None)
    down = list(range(levels - 1, -1, -1))
    orders = (tuple(down), tuple(down[:-2] + [0, 1]))

    def deal(t, hop):
        return pltpu.make_async_remote_copy(
            src_ref=send_ref.at[t, lax.rem(me + hop, n)],
            dst_ref=got.at[t, me],
            send_sem=deal_send.at[t, hop - 1],
            recv_sem=deal_recv.at[t, hop - 1],
            device_id={"row": lax.rem(me + hop, n)},
            device_id_type=MESH,
        )

    def swap_keys():
        return pltpu.make_async_remote_copy(
            src_ref=rem_keys.at[bits[0]],
            dst_ref=rem_keys.at[bits[0]],
            send_sem=key_send,
            recv_sem=key_recv,
            device_id={"row": across(me, bits[0], 0)},
            device_id_type=MESH,
        )

    def swap(t):
        return pltpu.make_async_remote_copy(
            src_ref=products.at[t, bits[0]],
            dst_ref=products.at[t, bits[0]],
            send_sem=send_sem.at[0, t],
            recv_sem=recv_sem.at[0, t],
            device_id={"row": across(me, bits[0], 0)},
            device_id_type=MESH,
        )

    def halve(t, b):
        where = (t,) + (every,) * (levels - b - 1) + (1 - bits[b],)
        return pltpu.make_async_remote_copy(
            src_ref=held[b - 1].at[where],
            dst_ref=landed[b - 1].at[t],
            send_sem=send_sem.at[b, t],
            recv_sem=recv_sem.at[b, t],
            device_id={"row": across(me, bits[b], b)},
            device_id_type=MESH,
        )

    def spread(t, j, order):
        done, b = order[:j], order[j]
        where = (t,) + tuple(every if c in done else bits[c] for c in down)
        return pltpu.make_async_remote_copy(
            src_ref=rem_out_ref.at[where],
            dst_ref=rem_out_ref.at[where],
            send_sem=send_sem.at[levels + j, t],
            recv_sem=recv_sem.at[levels + j, t],
            device_id={"row": across(me, bits[b], b)},
            device_id_type=MESH,
        )

    def by_order(t, act):
        last = lax.rem(t, 4) == 3
        for order, chosen in zip(orders, (jnp.logical_not(last), last)):

            @pl.when(chosen)
            def _():
                act(order)

    enter("row", n)

    def start_deal(t, carry):
        for hop in range(1, n):
            deal(t, hop).start()
        return carry

    lax.fori_loop(0, tables, start_deal, 0)
    rem_keys[bits[0]] = rows_ref[:, 1:2, :]
    swap_keys().start()

    def pick(wanted, table_ref, t, count):
        total = jnp.zeros((slots, width), jnp.float32)
        chunk = min(count, 512)
        for first in range(0, count, chunk):
            hot = one_hot(wanted, first, (slots, chunk), 1)
            total += jnp.dot(
                hot, table_ref[t, pl.ds(first, chunk), :], preferred_element_type=jnp.float32
            )
        return total

    def table_step(t):
        got[t, me] = send_ref[t, me]
        for hop in range(1, n):
            deal(t, hop).wait_recv()
        grads = got[t].reshape(slots, width).astype(jnp.float32)
        rows = rows_ref[t]
        cols = [jnp.broadcast_to(rows[i : i + 1, :], (width, slots)).T[:, 0:1] for i in range(2)]
        quot_pick = pick(cols[0], slab_ref, t, quot_rows)
        for_rem = (grads * quot_pick).astype(jnp.bfloat16)
        products[t, bits[0]] = for_rem
        swap(t).start()
        rem_pick = pick(cols[1], rem_ref, t, rem_rows)
        for_quot = (grads * rem_pick).astype(jnp.bfloat16)
        chunk = min(quot_rows, 512)
        for first in range(0, quot_rows, chunk):
            here = pl.ds(first, chunk)
            hot = one_hot(rows[0:1, :], first, (chunk, slots), 0)
            grad = jnp.dot(hot, for_quot, preferred_element_type=jnp.float32)
            fresh, fresh_acc = adagrad(slab_ref[t, here, :], qacc_ref[t, :, here], grad)
            quot_ref[t, here, :] = fresh
            qacc_out_ref[t, :, here] = fresh_acc

    def adagrad(old, accum, grad):
        count = old.shape[0]
        mean = jnp.mean(grad * grad, axis=-1, keepdims=True)
        fresh_acc = jnp.broadcast_to(accum, (width, count)).T + mean
        fresh = old.astype(jnp.float32) - step_rate * grad * lax.rsqrt(fresh_acc + epsilon)
        return fresh.astype(jnp.bfloat16), fresh_acc.T[0:1, :]

    def sum_of(t, b, where):
        kept = held[b - 1][(t,) + where + (bits[b],)].astype(jnp.float32)
        return kept + landed[b - 1][(t,) + where].astype(jnp.float32)

    def half_grad(t):
        for j in range(0, n // 2, 2):
            firsts = [(2 * (j + i) + bits[0]) * share for i in range(2)]
            grad = jnp.zeros((2 * share, width), jnp.float32)
            for side in range(2):
                keys = rem_keys[side, t]
                hots = [one_hot(keys, first, (share, slots), 0) for first in firsts]
                hot = jnp.concatenate(hots, axis=0)
                grad += jnp.dot(hot, products[t, side], preferred_element_type=jnp.float32)
            for i in range(2):
                where = tuple(((j + i) >> b) & 1 for b in range(levels - 2, -1, -1))
                held[0][(t,) + where] = grad[i * share : (i + 1) * share].astype(jnp.bfloat16)

    def comm_step(t, s):
        if s == 1:
            pl.when(t == 0)(lambda: swap_keys().wait_recv())
            swap(t).wait_recv()
            half_grad(t)
            halve(t, 1).start()
        elif s <= levels:
            halve(t, s - 1).wait_recv()
            if s < levels:
                for i in range(1 << (levels - s)):
                    where = tuple((i >> b) & 1 for b in range(levels - s - 1, -1, -1))
                    held[s - 1][(t,) + where] = sum_of(t, s - 1, where).astype(jnp.bfloat16)
                halve(t, s).start()
            else:
                mine = pl.ds(pl.multiple_of(me * share, share), share)
                accum = racc_ref[t, :, mine]
                fresh, fresh_acc = adagrad(rem_ref[t, mine, :], accum, sum_of(t, s - 1, ()))
                rem_out_ref[(t,) + tuple(bits[::-1])] = fresh
                racc_out_ref[t] = fresh_acc
                by_order(t, lambda order: spread(t, 0, order).start())
        else:
            j = s - levels - 1

            def pass_on(order):
                spread(t, j, order).wait_recv()
                if j < levels - 1:
                    spread(t, j + 1, order).start()

            by_order(t, pass_on)

    def step(i, carry):
        @pl.when(i < tables)
        def _():
            table_step(i)

        for s in range(2 * levels, 0, -1):
            t = i - s

            @pl.when((t >= 0) & (t < tables))
            def _():
                comm_step(t, s)

        return carry

    lax.fori_loop(0, tables + 2 * levels, step, 0)

    def finish(t, carry):
        for hop in range(1, n):
            deal(t, hop).wait_send()
        swap(t).wait_send()
        for b in range(1, levels):
            halve(t, b).wait_send()

        def sent(order):
            for j in range(levels):
                spread(t, j, order).wait_send()

        by_order(t, sent)
        return carry

    lax.fori_loop(0, tables, finish, 0)
    swap_keys().wait_send()


def tables_call(send_rows, keys, slab, qacc, rem_table, rem_accum):
    tables, n, capacity, width = send_rows.shape
    levels = n.bit_length() - 1
    rem_rows, quot_rows = rem_table.shape[1], slab.shape[1]
    share = rem_rows // n
    both = jnp.stack((keys // rem_rows, keys % rem_rows), axis=1)
    vmem = pl.BlockSpec(memory_space=pltpu.VMEM)
    cube = lambda b: (tables,) + (2,) * b + (share, width)
    outs = pl.pallas_call(
        functools.partial(tables_kernel, n, levels),
        out_shape=(
            jax.ShapeDtypeStruct(slab.shape, jnp.bfloat16),
            jax.ShapeDtypeStruct((tables, 1, quot_rows), jnp.float32),
            jax.ShapeDtypeStruct(cube(levels), jnp.bfloat16),
            jax.ShapeDtypeStruct((tables, 1, share), jnp.float32),
        ),
        in_specs=[vmem] * 6,
        out_specs=(vmem,) * 4,
        scratch_shapes=[pltpu.VMEM((tables, n, capacity, width), jnp.bfloat16)]
        + [
            pltpu.VMEM((2, tables, 1, n * capacity), jnp.int32),
            pltpu.VMEM((tables, 2, n * capacity, width), jnp.bfloat16),
        ]
        + [pltpu.VMEM(cube(b), jnp.bfloat16) for b in range(levels - 1, 0, -1)]
        + [pltpu.VMEM(cube(b), jnp.bfloat16) for b in range(levels - 2, -1, -1)]
        + [pltpu.SemaphoreType.DMA(())] * 2
        + [pltpu.SemaphoreType.DMA((tables, n - 1))] * 2
        + [pltpu.SemaphoreType.DMA((2 * levels, tables))] * 2,
        compiler_params=pltpu.CompilerParams(
            collective_id=0, has_side_effects=True, vmem_limit_bytes=60 << 20
        ),
    )(
        send_rows,
        both,
        slab,
        qacc[:, None, :],
        rem_table,
        rem_accum[:, None, :],
    )
    quot_out, quot_acc_out, rem_out, rem_acc_out = outs
    return (
        quot_out,
        quot_acc_out[:, 0],
        rem_out.reshape(rem_table.shape),
        rem_acc_out[:, 0],
    )


def rank_kernel(
    n_row,
    n,
    levels,
    feats_ref,
    cotan_ref,
    in_ref,
    out_ref,
    bias_ref,
    keys_ref,
    pooled_ref,
    got_ref,
    part,
    full,
    *rest,
):
    held = list(rest[: levels - 1])
    landed = list(rest[levels - 1 : 2 * levels - 1])
    deal_send, deal_recv, send_sem, recv_sem = rest[2 * levels - 1 :]
    row = lax.axis_index("row")
    me = lax.axis_index("table")
    bits = digits(me, levels)
    every = slice(None)
    stages = [part] + held
    samples = feats_ref.shape[0]
    rank = in_ref.shape[1]
    share = samples // n

    def deal(hop):
        return pltpu.make_async_remote_copy(
            src_ref=keys_ref.at[lax.rem(row + hop, n_row)],
            dst_ref=got_ref.at[row],
            send_sem=deal_send.at[hop - 1],
            recv_sem=deal_recv.at[hop - 1],
            device_id={"row": lax.rem(row + hop, n_row)},
            device_id_type=MESH,
        )

    def halve(t, b):
        where = (t,) + (every,) * (levels - b - 1) + (1 - bits[b],)
        return pltpu.make_async_remote_copy(
            src_ref=stages[b].at[where],
            dst_ref=landed[b].at[t],
            send_sem=send_sem.at[b, t],
            recv_sem=recv_sem.at[b, t],
            device_id={"table": across(me, bits[b], b)},
            device_id_type=MESH,
        )

    def spread(t, b):
        where = (t,) + (every,) * (levels - b - 1) + tuple(bits[c] for c in range(b, -1, -1))
        return pltpu.make_async_remote_copy(
            src_ref=full.at[where],
            dst_ref=full.at[where],
            send_sem=send_sem.at[levels + b, t],
            recv_sem=recv_sem.at[levels + b, t],
            device_id={"table": across(me, bits[b], b)},
            device_id_type=MESH,
        )

    barrier = pltpu.get_barrier_semaphore()
    for axis, size, at in (("table", n, me), ("row", n_row, row)):
        for hop in range(1, size):
            pl.semaphore_signal(
                barrier, inc=1, device_id={axis: lax.rem(at + hop, size)}, device_id_type=MESH
            )
    pl.semaphore_wait(barrier, n + n_row - 2)
    for hop in range(1, n_row):
        deal(hop).start()

    def project(t, source, weight_ref):
        partial = jnp.dot(source, weight_ref[...], preferred_element_type=jnp.float32)
        part[t] = partial.astype(jnp.bfloat16).reshape(part.shape[1:])
        halve(t, 0).start()

    feats = feats_ref[...]
    cotan = cotan_ref[...].astype(jnp.float32)
    project(0, feats, in_ref)
    project(1, (cotan * feats.astype(jnp.float32)).astype(jnp.bfloat16), out_ref)
    got_ref[row] = keys_ref[row]
    for b in range(levels):
        for t in range(2):
            halve(t, b).wait_recv()
            mine = stages[b][(t,) + (every,) * (levels - b - 1) + (bits[b],)].astype(jnp.float32)
            total = (mine + landed[b][t].astype(jnp.float32)).astype(jnp.bfloat16)
            if b < levels - 1:
                held[b][t] = total
                halve(t, b + 1).start()
            else:
                full[(t,) + tuple(bits[::-1])] = total
                spread(t, b).start()
    for b in range(levels - 1, 0, -1):
        for t in range(2):
            spread(t, b).wait_recv()
            spread(t, b - 1).start()
    contract = (((1,), (1,)), ((), ()))
    back = []
    for t, weight_ref in ((0, out_ref), (1, in_ref)):
        spread(t, 0).wait_recv()
        whole = full[t].reshape(samples, rank)
        back.append(
            lax.dot_general(whole, weight_ref[...], contract, preferred_element_type=jnp.float32)
        )
    pooled = cotan * (back[0] + bias_ref[...] + 1.0) + back[1]
    pooled_ref[...] = pooled.astype(jnp.bfloat16)
    for hop in range(1, n_row):
        deal(hop).wait()
    for t in range(2):
        for b in range(levels):
            halve(t, b).wait_send()
            spread(t, b).wait_send()


def rank_call(features, cotangent, cross_in, cross_out, bias, keys):
    n_row, n = lax.axis_size("row"), lax.axis_size("table")
    levels = n.bit_length() - 1
    samples, columns = features.shape
    share, rank = samples // n, cross_in.shape[1]
    vmem = pl.BlockSpec(memory_space=pltpu.VMEM)
    cube = lambda b: pltpu.VMEM((2,) + (2,) * b + (share, rank), jnp.bfloat16)
    return pl.pallas_call(
        functools.partial(rank_kernel, n_row, n, levels),
        out_shape=(
            jax.ShapeDtypeStruct((samples, columns), jnp.bfloat16),
            jax.ShapeDtypeStruct(keys.shape, jnp.int32),
        ),
        in_specs=[vmem] * 6,
        out_specs=(vmem,) * 2,
        scratch_shapes=[cube(levels), cube(levels)]
        + [cube(b) for b in range(levels - 1, 0, -1)]
        + [cube(b) for b in range(levels - 1, -1, -1)]
        + [pltpu.SemaphoreType.DMA((n_row - 1,))] * 2
        + [pltpu.SemaphoreType.DMA((2 * levels, 2))] * 2,
        compiler_params=pltpu.CompilerParams(
            collective_id=1, has_side_effects=True, vmem_limit_bytes=60 << 20
        ),
    )(features, cotangent, cross_in, cross_out, bias[None, :], keys)


def per_device(
    features,
    cotangent,
    cross_in,
    cross_out,
    bias,
    dest_shard,
    quot_row,
    rem_row,
    quot_slab,
    quot_accum,
    rem_table,
    rem_accum,
):
    samples = features.shape[0]
    tables_dev = quot_slab.shape[0]
    row_width = quot_slab.shape[2]
    rem_rows = rem_table.shape[1]
    row_count = lax.axis_size("row")
    capacity = 3 * samples // (2 * row_count)
    slots = row_count * capacity
    target = dest_shard[:, :, 0]
    onehot = target[:, :, None] == jnp.arange(row_count, dtype=jnp.int32)[None, None, :]
    lower = (
        jnp.arange(samples, dtype=jnp.int32)[:, None]
        >= jnp.arange(samples, dtype=jnp.int32)[None, :]
    ).astype(jnp.bfloat16)
    running = jnp.einsum(
        "ij,tjn->tin", lower, onehot.astype(jnp.bfloat16), preferred_element_type=jnp.float32
    )
    slot_index = jnp.sum(jnp.where(onehot, running, 0.0), axis=2).astype(jnp.int32) - 1
    position = target * capacity + slot_index
    placed = position[:, :, None] == jnp.arange(slots, dtype=jnp.int32)[None, None, :]
    key_words = quot_row * rem_rows + rem_row
    send_keys = jnp.sum(jnp.where(placed, key_words[:, :, None], 0), axis=1)
    send_keys = send_keys.reshape(tables_dev, row_count, capacity).transpose(1, 0, 2)
    pooled, got_keys = rank_call(features, cotangent, cross_in, cross_out, bias, send_keys)
    pooled = pooled.reshape(samples, tables_dev, row_width)
    send_rows = jnp.einsum(
        "tsk,ste->tke", placed.astype(jnp.bfloat16), pooled, preferred_element_type=jnp.float32
    ).astype(jnp.bfloat16)
    send_rows = send_rows.reshape(tables_dev, row_count, capacity, row_width)
    got_keys = got_keys.transpose(1, 0, 2).reshape(tables_dev, slots)
    return tables_call(send_rows, got_keys, quot_slab, quot_accum, rem_table, rem_accum)


def solution(mesh):
    placed = (
        P("row", "table"),
        P("row", "table"),
        P("table", None),
        P("table", None),
        P("table"),
        P("table", "row", None),
        P("table", "row"),
        P("table", "row"),
        P("table", "row", None),
        P("table", "row"),
        P("table", None, None),
        P("table", None),
    )
    return jax.shard_map(
        per_device,
        mesh=mesh,
        in_specs=placed,
        out_specs=(
            P("table", "row", None),
            P("table", "row"),
            P("table", None, None),
            P("table", "row"),
        ),
        check_vma=False,
    )
```
